512 devices in a mesh: span: 64 (over x, z), head: 8 (over y, core).
Axes of the slice: x: 4, y: 4, z: 16, core: 2. Of those that a mesh axis runs over, the one named last changes fastest.
Arguments:
- queries: bfloat16 [16384, 8192], P('span', 'head'), may hold values from -15 to 15
- keys: bfloat16 [16384, 1024], P(('span', 'head')), may hold values from -8 to 8
- values: bfloat16 [16384, 1024], P(('span', 'head')), may hold values from -6 to 6
- parent: int32 [32], replicated, may hold values from -1 to 15, as said below
- owner: int32 [32], replicated, may hold values from 0 to 31, each once
- lengths: int32 [32], replicated, may hold values from 1 to 512, as said below
Outputs:
- attended: bfloat16 [16384, 8192], P('span', 'head')
The draws below stay inside these ranges and needn't reach their ends.
Inputs may be any that keep to these rules, and one draw needn't show every extreme that they name: Spans are numbered level by level from the roots down, with 4, 4, 8 and 16 spans on the four levels; a span's parent lies on the level above it, every span above the lowest level has a child, and no span has more than 3 ancestors. `owner`: each slot holds one span. `lengths`: every span that has a child holds 512 valid tokens; a span's valid tokens are its first ones.
All inputs are finite; a program needn't handle non-finite values.
Results may differ from the reference program's by a relative error of at most 0.0065.
Values may be sent and summed in bfloat16 or wider, within the bound.
No kernel may reach another device: no remote copies, remote signals or barrier semaphores. Data moves between devices by JAX's collectives and lax.ppermute only.
A program may use at most 64 MiB of HBM per device.

```python
import jax
import jax.numpy as jnp
from jax import lax

QH = 64
KVH = 8
HD = 128
SPAN_LEN = 512
SPANS = 32
TOKENS = 16384


def draw_queries(key, part):
    key = jax.random.fold_in(key, 1)
    entries = jnp.clip(2.5 * jax.random.normal(key, (TOKENS, QH * HD), jnp.float32), -15.0, 15.0)
    return entries.astype(jnp.bfloat16)


def draw_keys(key, part):
    key = jax.random.fold_in(key, 3)
    entries = jnp.clip(jax.random.normal(key, (TOKENS, KVH * HD), jnp.float32), -6.0, 6.0)
    return entries.astype(jnp.bfloat16)


def draw_parent(key, part):
    key = jax.random.fold_in(key, 11)
    span_ids = jnp.arange(SPANS, dtype=jnp.int32)
    first_cut = SPANS // 8
    second_boundary = SPANS // 4
    third_cut = SPANS // 2
    height = (span_ids >= first_cut).astype(jnp.int32) + (span_ids >= second_boundary).astype(jnp.int32) + (span_ids >= third_cut).astype(jnp.int32)
    above_start = jnp.where(height == 1, 0, jnp.where(height == 2, first_cut, second_boundary))
    above_count = jnp.where(height == 1, first_cut, jnp.where(height == 2, second_boundary - first_cut, third_cut - second_boundary))
    own_start = jnp.where(height == 1, first_cut, jnp.where(height == 2, second_boundary, third_cut))
    inside_offset = span_ids - own_start
    random_pick = jax.random.randint(key, (SPANS,), 0, SPANS, dtype=jnp.int32) % jnp.maximum(above_count, 1)
    picked = jnp.where(inside_offset < above_count, inside_offset, random_pick)
    return jnp.where(height == 0, -1, above_start + picked).astype(jnp.int32)


def draw_lengths(key, part):
    key = jax.random.fold_in(key, 13)
    span_ids = jnp.arange(SPANS, dtype=jnp.int32)
    drawn = 1 + jax.random.randint(key, (SPANS,), 0, SPAN_LEN, dtype=jnp.int32)
    drawn = jnp.where(span_ids == SPANS // 2, 1, drawn)
    return jnp.where(span_ids < SPANS // 2, SPAN_LEN, drawn).astype(jnp.int32)


def block_scale(rng, extent, split, low, high):
    def one(dim, parts):
        steps = jax.random.uniform(jax.random.fold_in(jax.random.fold_in(rng, 6), dim), (parts,), jnp.float32, low / len(split), high / len(split))
        return jnp.repeat(jnp.exp(steps), extent[dim] // parts).reshape((-1,) + (1,) * (len(extent) - dim - 1))

    gain = one(*split[0])
    for cut in split[1:]:
        gain = gain * one(*cut)
    return gain


def bell_draw(stream_key, extent, deviation, reach, cuts=(), held_as=jnp.bfloat16):
    values = jax.random.normal(stream_key, extent, jnp.float32) * deviation
    if len(cuts) > 0:
        values = block_scale(stream_key, extent, cuts, -0.22, 0.18) * values
    return jnp.clip(values, min=-reach, max=reach).astype(held_as)


def setup_inputs(seed: int = 0) -> dict:
    key_of = jax.random.split(jax.random.key(seed), 7)
    return {
        "queries": draw_queries(jax.random.fold_in(key_of[6], 71), 0),
        "keys": draw_keys(jax.random.fold_in(key_of[6], 71), 0),
        "values": bell_draw(key_of[2], (TOKENS, KVH * HD), 1.0, 6.0, ((0, 512),)),
        "parent": draw_parent(jax.random.fold_in(key_of[6], 71), 0),
        "owner": jax.random.permutation(key_of[4], SPANS).astype(jnp.int32),
        "lengths": draw_lengths(jax.random.fold_in(key_of[6], 71), 0),
    }


def reference(queries, keys, values, parent, owner, lengths):
    repeats = QH // KVH
    scale_factor = HD ** -0.5
    span_ids = jnp.arange(SPANS, dtype=jnp.int32)
    token_ids = jnp.arange(SPAN_LEN, dtype=jnp.int32)
    causal = token_ids[:, None] >= token_ids[None, :]

    def one_slot(slot_index):
        held_span = jnp.sum(jnp.where(owner == slot_index, span_ids, 0)).astype(jnp.int32)
        anchors = []
        present_flags = []
        current = held_span
        for height in range(3):
            upward = parent[jnp.maximum(current, 0)]
            current = jnp.where(current >= 0, upward, -1).astype(jnp.int32)
            anchors.append(owner[jnp.maximum(current, 0)].astype(jnp.int32))
            present_flags.append(jnp.broadcast_to(current >= 0, (SPAN_LEN, SPAN_LEN)))
        anchors.append(slot_index)
        key_rows = jnp.concatenate([lax.dynamic_slice_in_dim(keys, anchor * SPAN_LEN, SPAN_LEN, 0) for anchor in anchors], axis=0)
        value_rows = jnp.concatenate([lax.dynamic_slice_in_dim(values, anchor * SPAN_LEN, SPAN_LEN, 0) for anchor in anchors], axis=0)
        query_rows = lax.dynamic_slice_in_dim(queries, slot_index * SPAN_LEN, SPAN_LEN, 0).reshape(SPAN_LEN, KVH, repeats, HD)
        visible = jnp.concatenate(present_flags + [causal], axis=1)
        key_head_total = key_rows.reshape(4 * SPAN_LEN, KVH, HD)
        value_heads = value_rows.reshape(4 * SPAN_LEN, KVH, HD)

        def one_head(kv_group):
            query_head = lax.dynamic_index_in_dim(query_rows, kv_group, 1, keepdims=False).astype(jnp.float32)
            key_head = lax.dynamic_index_in_dim(key_head_total, kv_group, 1, keepdims=False).astype(jnp.float32)
            value_head = lax.dynamic_index_in_dim(value_heads, kv_group, 1, keepdims=False).astype(jnp.float32)
            scores = jnp.einsum("trd,sd->rts", query_head, key_head) * scale_factor
            scores = jnp.where(visible, scores, -jnp.inf)
            row_top = jnp.max(scores, axis=-1, keepdims=True)
            weights = jnp.exp(scores - row_top)
            weight_total = jnp.sum(weights, axis=-1)
            rounded = weights.astype(jnp.bfloat16)
            summed = jnp.einsum("rts,sd->rtd", rounded.astype(jnp.float32), value_head)
            return summed / weight_total[..., None]

        per_head = lax.map(one_head, jnp.arange(KVH, dtype=jnp.int32))
        merged = per_head.transpose(2, 0, 1, 3).reshape(SPAN_LEN, QH * HD)
        valid_rows = token_ids < lengths[held_span]
        return jnp.where(valid_rows[:, None], merged, 0.0).astype(jnp.bfloat16)

    blocks = lax.map(one_slot, jnp.arange(SPANS, dtype=jnp.int32))
    return blocks.reshape(TOKENS, QH * HD)
```

```python
import functools

import jax
import jax.numpy as jnp
from jax import lax
from jax.experimental import pallas as pl
from jax.experimental.pallas import tpu as pltpu
from jax.sharding import Mesh, PartitionSpec as P

HD = 128
HEADS = 8
HALF = 256
CHUNK = 32
PIECE = 16
SLOTS = 32
LEVELS = 3
EXP_FACTOR = HD ** (-0.5) * 1.4426950408889634

VMEM = pl.BlockSpec(memory_space=pltpu.VMEM)
SMEM = pl.BlockSpec(memory_space=pltpu.SMEM)


def pack_kernel(keys_ref, values_ref, out_ref):
    for head in range(HEADS):
        columns = pl.ds(head * HD, HD)
        for kind, ref in enumerate((keys_ref, values_ref)):
            block = ref[:, columns]
            out_ref[head, kind] = block
            out_ref[HEADS + head, kind] = block


def split_kernel(own_ref, out_ref):
    half = lax.axis_index("zl")
    for head in range(HEADS):
        for kind in range(2):
            block = own_ref[half * HEADS + head, kind]
            first = kind * (HALF // PIECE) + head * 2
            out_ref[pl.ds(first, 2)] = block.reshape(2, PIECE, HD)


def pick_kernel(parent_ref, owner_ref, spread_ref, out_ref, span_at_ref):
    for span in range(SLOTS):
        span_at_ref[owner_ref[span]] = span
    for slot in range(SLOTS):
        current = span_at_ref[slot]
        for level in range(LEVELS):
            current = jnp.where(current >= 0, parent_ref[jnp.maximum(current, 0)], -1)
            source = owner_ref[jnp.maximum(current, 0)]
            out_ref[slot, level] = spread_ref[source]


def attend_kernel(parent_ref, owner_ref, lengths_ref, queries_ref, own_ref, near_ref, far_ref, out_ref):
    half = lax.axis_index("zl")
    my_slot = lax.axis_index("x") * 8 + lax.axis_index("zh")
    my_span = jnp.int32(0)
    for span in range(SLOTS):
        my_span = jnp.where(owner_ref[span] == my_slot, span, my_span)
    local_length = lengths_ref[my_span]
    count = jnp.int32(0)
    current = my_span
    for _ in range(LEVELS):
        current = jnp.where(current >= 0, parent_ref[jnp.maximum(current, 0)], -1)
        count = count + jnp.where(current >= 0, 1, 0)

    row_ids = lax.broadcasted_iota(jnp.int32, (HALF, HALF), 0)
    column_ids = lax.broadcasted_iota(jnp.int32, (HALF, HALF), 1)

    def own_rows(which, kind):
        return own_ref[pl.ds(which * HEADS, HEADS), kind].reshape(HALF, HD)

    def piece_rows(ref, level, kind):
        return ref[pl.ds(kind * 16, 16), level].reshape(HALF, HD)

    def body(levels, second):
        def key_blocks(kind):
            if second:
                yield own_rows(1, kind)
                yield own_rows(0, kind)
            else:
                yield own_rows(0, kind)
            for level in range(levels):
                yield piece_rows(near_ref, level, kind)
                yield piece_rows(far_ref, level, kind)

        def one_head(head, carry):
            columns = pl.ds(pl.multiple_of(head * HD, HD), HD)
            query = queries_ref[:, columns]
            scores = []
            for index, block in enumerate(key_blocks(0)):
                part = lax.dot_general(
                    query, block, (((1,), (1,)), ((), ())), preferred_element_type=jnp.float32
                )
                if index == 0:
                    part = jnp.where(row_ids >= column_ids, part, -jnp.inf)
                scores.append(part)
            top = functools.reduce(jnp.maximum, scores)
            top = jnp.max(top, axis=1, keepdims=True)
            total = None
            summed = None
            for part, block in zip(scores, key_blocks(1)):
                weights = jnp.exp2((part - top) * EXP_FACTOR)
                total = weights if total is None else total + weights
                product = jnp.dot(
                    weights.astype(jnp.bfloat16), block, preferred_element_type=jnp.float32
                )
                summed = product if summed is None else summed + product
            total = jnp.sum(total, axis=1, keepdims=True)
            result = summed / total
            positions = half * HALF + lax.broadcasted_iota(jnp.int32, (HALF, HD), 0)
            result = jnp.where(positions < local_length, result, 0.0)
            out_ref[:, columns] = result.astype(jnp.bfloat16)
            return carry

        lax.fori_loop(0, HEADS, one_head, 0)

    for levels in range(LEVELS + 1):
        for second in (False, True):

            @pl.when((count == levels) & (half == (1 if second else 0)))
            def _(levels=levels, second=second):
                body(levels, second)


def on_device(queries, keys, values, parent, owner, lengths):
    bf16 = jnp.bfloat16
    packed = pl.pallas_call(
        pack_kernel,
        out_shape=jax.ShapeDtypeStruct((16, 2, CHUNK, HD), bf16),
        in_specs=[VMEM, VMEM],
        out_specs=VMEM,
        name="pack_heads",
    )(keys, values)
    own = lax.all_to_all(packed, ("zl", "y", "c"), 0, 0, tiled=True)
    pieces = pl.pallas_call(
        split_kernel,
        out_shape=jax.ShapeDtypeStruct((SLOTS, PIECE, HD), bf16),
        in_specs=[VMEM],
        out_specs=VMEM,
        name="split_half",
    )(own)
    spread = lax.all_to_all(pieces, ("x", "zh"), 0, 0, tiled=True)
    picked = pl.pallas_call(
        pick_kernel,
        out_shape=jax.ShapeDtypeStruct((SLOTS, LEVELS, PIECE, HD), bf16),
        in_specs=[SMEM, SMEM, VMEM],
        out_specs=VMEM,
        scratch_shapes=[pltpu.SMEM((SLOTS,), jnp.int32)],
        name="pick_ancestors",
    )(parent, owner, spread)
    near = lax.all_to_all(picked, ("x", "zh"), 0, 0, tiled=True)
    far = lax.ppermute(near, "zl", [(0, 1), (1, 0)])
    return pl.pallas_call(
        attend_kernel,
        out_shape=jax.ShapeDtypeStruct((HALF, HEADS * HD), bf16),
        in_specs=[SMEM, SMEM, SMEM, VMEM, VMEM, VMEM, VMEM],
        out_specs=VMEM,
        compiler_params=pltpu.CompilerParams(vmem_limit_bytes=32 * 1024 * 1024),
        name="attend",
    )(parent, owner, lengths, queries, own, near, far)


def solution(mesh):
    fine = Mesh(mesh.devices.reshape(4, 8, 2, 4, 2), ("x", "zh", "zl", "y", "c"))
    span, head = ("x", "zh", "zl"), ("y", "c")
    return jax.shard_map(
        on_device,
        mesh=fine,
        in_specs=(P(span, head), P(span + head, None), P(span + head, None), P(), P(), P()),
        out_specs=P(span, head),
        check_vma=False,
    )
```

```python
import functools

import jax
import jax.numpy as jnp
from jax import lax
from jax.experimental import pallas as pl
from jax.experimental.pallas import tpu as pltpu
from jax.sharding import Mesh, PartitionSpec as P

HD = 128
HEADS = 8
HALF = 256
SPANS = 32
LEVELS = 3
PLACES = 8
STRIP = 8
SHARE = HEADS * STRIP
TABLE = 8
ROW = 128
HIDDEN = -1e30
EXP_FACTOR = HD ** (-0.5) * 1.4426950408889634

VMEM = pl.BlockSpec(memory_space=pltpu.VMEM)
SMEM = pl.BlockSpec(memory_space=pltpu.SMEM)


def pack_kernel(parent_ref, owner_ref, lengths_ref, keys_ref, values_ref, out_ref, facts_ref, span_at_ref):
    for kind, ref in enumerate((keys_ref, values_ref)):
        for strip in range(4):
            rows = ref[pl.ds(strip * STRIP, STRIP), :]
            for head in range(HEADS):
                columns = rows[:, head * HD : (head + 1) * HD]
                out_ref[kind * 2 + strip // 2, strip % 2, pl.ds(head * STRIP, STRIP), :] = columns
    half = lax.axis_index("zl")
    pair = lax.axis_index("zb") * 2 + lax.axis_index("i")
    mine = lax.axis_index("x")
    beside = (pair + 7 + half * 2) & 7
    for span in range(SPANS):
        span_at_ref[owner_ref[span]] = span
    my_count = jnp.int32(0)
    my_length = jnp.int32(0)
    for x in range(4):
        for side in range(2):
            slot = x * 8 + (pair if side == 0 else beside)
            current = span_at_ref[slot]
            length = lengths_ref[current]
            count = jnp.int32(0)
            entry = TABLE + (x * 2 + side) * (1 + LEVELS)
            facts_ref[entry] = ((slot >> 1) & 3) * PLACES + (slot >> 3) * 2 + (slot & 1)
            for level in range(LEVELS):
                current = jnp.where(current >= 0, parent_ref[jnp.maximum(current, 0)], -1)
                count = count + jnp.where(current >= 0, 1, 0)
                slot = owner_ref[jnp.maximum(current, 0)]
                facts_ref[entry + 1 + level] = ((slot >> 1) & 3) * PLACES + (slot >> 3) * 2 + (slot & 1)
            if side == 0:
                my_count = jnp.where(mine == x, count, my_count)
                my_length = jnp.where(mine == x, length, my_length)
    facts_ref[0] = my_count
    facts_ref[1] = my_length


def pick_kernel(facts_ref, gathered_ref, out_ref):
    for x in range(4):
        for side in range(2):
            for level in range(1 + LEVELS):
                source = facts_ref[TABLE + (x * 2 + side) * (1 + LEVELS) + level]
                out_ref[x, side, level] = gathered_ref[source]


def partial_attention(queries, keys, values, causal):
    all_scores = [
        lax.dot_general(keys, query, (((1,), (1,)), ((), ())), preferred_element_type=jnp.float32)
        for query in queries
    ]
    for scores in all_scores:
        if causal is not None:
            masked = jnp.where(causal, scores[:ROW], HIDDEN)
            scores = jnp.concatenate([masked, scores[ROW:]], axis=0) if scores.shape[0] > ROW else masked
        top = jnp.max(scores, axis=0, keepdims=True)
        weights = jnp.exp2((scores - top) * EXP_FACTOR)
        total = jnp.sum(weights, axis=0, keepdims=True)
        summed = lax.dot_general(
            values, weights.astype(jnp.bfloat16), (((0,), (0,)), ((), ())), preferred_element_type=jnp.float32
        )
        yield top, total, summed


def save(summed_ref, stats_ref, head, top, total, summed):
    summed_ref[head] = summed
    stats_ref[head, pl.ds(0, 8)] = jnp.broadcast_to(top, (8, HALF))
    stats_ref[head, pl.ds(8, 8)] = jnp.broadcast_to(total, (8, HALF))


def head_queries(queries_ref):
    return [queries_ref[:, head * HD : (head + 1) * HD] for head in range(HEADS)]


def chunk_rows(ref, kind, with_own, levels):
    blocks = []
    if with_own:
        blocks.append(ref[pl.ds(kind * 2, 2), 0].reshape(ROW, HD))
    if levels > 0:
        blocks.append(ref[pl.ds(kind * 2, 2), 1 : 1 + levels].reshape(levels * ROW, HD))
    return blocks


def causal_mask(source_i):
    rows = lax.broadcasted_iota(jnp.int32, (ROW, HALF), 1)
    spots = lax.broadcasted_iota(jnp.int32, (ROW, HALF), 0)
    key_rows = ((spots & 56) << 2) + ((spots >> 6) << 4) + (spots & 7)
    return rows >= key_rows + source_i * STRIP


def attend_kernel(begins, ends, near_count, far_count, facts_ref, queries_ref, *refs):
    chunk_count = near_count + far_count
    chunks, rest = refs[:chunk_count], refs[chunk_count:]
    state, outs = ((), rest) if begins else (rest[:2], rest[2:])
    half = lax.axis_index("zl")
    own_i = lax.axis_index("i")
    count = facts_ref[0]
    causal = causal_mask(own_i if begins else 1 - own_i) if near_count else None
    positions = half * HALF + lax.broadcasted_iota(jnp.int32, (HALF, HD), 0)
    valid = positions < facts_ref[1]

    def finish(head, top, total, summed):
        if ends:
            result = (summed * (1.0 / total)).T
            outs[0][:, head * HD : (head + 1) * HD] = jnp.where(valid, result, 0.0).astype(jnp.bfloat16)
        else:
            save(*outs, head, top, total, summed)

    def stored(head):
        return state[1][head, pl.ds(0, 8)][:1], state[1][head, pl.ds(8, 8)][:1], state[0][head]

    def body(levels, second):
        def rows_of(kind):
            blocks = []
            for index, chunk in enumerate(chunks):
                blocks += chunk_rows(chunk, kind, index < near_count or second, levels)
            return blocks

        if not rows_of(0):
            for head in range(HEADS):
                finish(head, *stored(head))
            return
        keys, values = (jnp.concatenate(rows_of(kind), axis=0) for kind in range(2))
        parts = partial_attention(head_queries(queries_ref), keys, values, causal)
        for head, (top2, total2, summed2) in enumerate(parts):
            if begins:
                finish(head, top2, total2, summed2)
                continue
            top, total, summed = stored(head)
            newest = jnp.maximum(top, top2)
            shrink = jnp.exp2((top - newest) * EXP_FACTOR)
            shrink2 = jnp.exp2((top2 - newest) * EXP_FACTOR)
            finish(head, newest, total * shrink + total2 * shrink2, summed * shrink + summed2 * shrink2)

    for levels in range(LEVELS + 1):
        if far_count == 0:
            pl.when(count == levels)(functools.partial(body, levels, False))
            continue
        for second in (False, True):
            here = (count == levels) & (half == (1 if second else 0))
            pl.when(here)(functools.partial(body, levels, second))


def on_device(queries, keys, values, parent, owner, lengths):
    bf16, f32 = jnp.bfloat16, jnp.float32
    params = pltpu.CompilerParams(vmem_limit_bytes=32 * 1024 * 1024)
    work = pl.CostEstimate(
        flops=4 * HEADS * HALF * HD * 1024, bytes_accessed=4 * 1024 * 1024, transcendentals=HEADS * HALF * 1024
    )
    small = pltpu.CompilerParams(vmem_limit_bytes=4 * 1024 * 1024)
    packed, facts = pl.pallas_call(
        pack_kernel,
        out_shape=[
            jax.ShapeDtypeStruct((4, 2, SHARE, HD), bf16),
            jax.ShapeDtypeStruct((TABLE + PLACES * (1 + LEVELS),), jnp.int32),
        ],
        in_specs=[SMEM, SMEM, SMEM, VMEM, VMEM],
        out_specs=[VMEM, SMEM],
        scratch_shapes=[pltpu.SMEM((SPANS,), jnp.int32)],
        name="pack_heads",
    )(parent, owner, lengths, keys, values)
    spread = lax.all_to_all(packed.reshape(64, STRIP, HD), ("x", "i", "y", "c"), 0, 0, tiled=True)
    gathered = lax.all_gather(spread.reshape(PLACES, SHARE, HD), "zb", axis=0, tiled=True)
    picked = pl.pallas_call(
        pick_kernel,
        out_shape=jax.ShapeDtypeStruct((4, 2, 1 + LEVELS, SHARE, HD), bf16),
        in_specs=[SMEM, VMEM],
        out_specs=VMEM,
        compiler_params=small,
        name="pick_ancestors",
    )(facts, gathered)
    passed = lax.all_to_all(picked, "x", 0, 0, tiled=True)
    ours, beside = passed[:, 0], passed[:, 1]
    ring = ("zb", "i", "zl")
    far = lax.ppermute(ours, ring, [(z, z ^ 1) for z in range(16)])
    further = lax.ppermute(beside, ring, [(z, (z + (1 if z % 2 else -1)) % 16) for z in range(16)])
    state = [jax.ShapeDtypeStruct((HEADS, HD, HALF), f32), jax.ShapeDtypeStruct((HEADS, 16, HALF), f32)]

    def attend(name, begins, ends, near_count, far_count, *operands):
        return pl.pallas_call(
            functools.partial(attend_kernel, begins, ends, near_count, far_count),
            out_shape=jax.ShapeDtypeStruct((HALF, HEADS * HD), bf16) if ends else state,
            in_specs=[SMEM] + [VMEM] * (1 + len(operands)),
            out_specs=VMEM if ends else [VMEM, VMEM],
            compiler_params=params,
            cost_estimate=work,
            name=name,
        )(facts, queries, *operands)

    running = attend("attend_own", True, False, 1, 0, ours)
    beside, running = lax.optimization_barrier((beside, running))
    near = lax.ppermute(beside, ring, [(z, (z + (2 if z % 2 else -2)) % 16) for z in range(16)])
    running = attend("attend_middle", False, False, 0, 2, far, further, *running)
    return attend("attend_last", False, True, 1, 0, near, *running)


def solution(mesh):
    fine = Mesh(mesh.devices.reshape(4, 4, 2, 2, 4, 2), ("x", "zb", "i", "zl", "y", "c"))
    span, head = ("x", "zb", "i", "zl"), ("y", "c")
    return jax.shard_map(
        on_device,
        mesh=fine,
        in_specs=(P(span, head), P(span + head, None), P(span + head, None), P(), P(), P()),
        out_specs=P(span, head),
        check_vma=False,
    )
```

```python
import functools

import jax
import jax.numpy as jnp
from jax import lax
from jax.experimental import pallas as pl
from jax.experimental.pallas import tpu as pltpu
from jax.sharding import Mesh, PartitionSpec as P

HD = 128
HEADS = 8
HALF = 256
SPANS = 32
LEVELS = 3
PLACES = 8
STRIP = 8
SHARE = HEADS * STRIP
TABLE = 8
ROW = 128
HIDDEN = -1e30
EXP_FACTOR = HD ** (-0.5) * 1.4426950408889634

VMEM = pl.BlockSpec(memory_space=pltpu.VMEM)
SMEM = pl.BlockSpec(memory_space=pltpu.SMEM)


def pack_kernel(parent_ref, owner_ref, lengths_ref, keys_ref, values_ref, out_ref, facts_ref, span_at_ref):
    for kind, ref in enumerate((keys_ref, values_ref)):
        for part in range(2):
            for head in range(HEADS):
                out_ref[kind * 2 + part, head] = ref[pl.ds(part * 16, 16), pl.ds(head * HD, HD)]
    half = lax.axis_index("zl")
    pair = lax.axis_index("zb") * 2 + lax.axis_index("i")
    mine = lax.axis_index("x")
    beside = (pair + 7 + half * 2) & 7
    for span in range(SPANS):
        span_at_ref[owner_ref[span]] = span
    my_count = jnp.int32(0)
    my_length = jnp.int32(0)
    for x in range(4):
        for side in range(2):
            slot = x * 8 + (pair if side == 0 else beside)
            current = span_at_ref[slot]
            length = lengths_ref[current]
            count = jnp.int32(0)
            entry = TABLE + (x * 2 + side) * (1 + LEVELS)
            facts_ref[entry] = ((slot >> 1) & 3) * PLACES + (slot >> 3) * 2 + (slot & 1)
            for level in range(LEVELS):
                current = jnp.where(current >= 0, parent_ref[jnp.maximum(current, 0)], -1)
                count = count + jnp.where(current >= 0, 1, 0)
                slot = owner_ref[jnp.maximum(current, 0)]
                facts_ref[entry + 1 + level] = ((slot >> 1) & 3) * PLACES + (slot >> 3) * 2 + (slot & 1)
            if side == 0:
                my_count = jnp.where(mine == x, count, my_count)
                my_length = jnp.where(mine == x, length, my_length)
    facts_ref[0] = my_count
    facts_ref[1] = my_length


def pick_kernel(facts_ref, gathered_ref, out_ref):
    for x in range(4):
        for side in range(2):
            for level in range(1 + LEVELS):
                source = facts_ref[TABLE + (x * 2 + side) * (1 + LEVELS) + level]
                out_ref[x, side, level] = gathered_ref[source >> 1, :, source & 1]


def partial_attention(queries, keys, values, causal):
    all_scores = [
        lax.dot_general(keys, query, (((1,), (1,)), ((), ())), preferred_element_type=jnp.float32)
        for query in queries
    ]
    for scores in all_scores:
        if causal is not None:
            masked = jnp.where(causal, scores[:ROW], HIDDEN)
            scores = jnp.concatenate([masked, scores[ROW:]], axis=0) if scores.shape[0] > ROW else masked
        top = jnp.max(scores, axis=0, keepdims=True)
        weights = jnp.exp2((scores - top) * EXP_FACTOR)
        total = jnp.sum(weights, axis=0, keepdims=True)
        summed = lax.dot_general(
            values, weights.astype(jnp.bfloat16), (((0,), (0,)), ((), ())), preferred_element_type=jnp.float32
        )
        yield top, total, summed


def save(summed_ref, stats_ref, head, top, total, summed):
    summed_ref[head] = summed
    stats_ref[head, pl.ds(0, 8)] = jnp.broadcast_to(top, (8, HALF))
    stats_ref[head, pl.ds(8, 8)] = jnp.broadcast_to(total, (8, HALF))


def head_queries(queries_ref):
    return [queries_ref[:, head * HD : (head + 1) * HD] for head in range(HEADS)]


def chunk_rows(ref, kind, with_own, levels):
    blocks = []
    if with_own:
        blocks.append(ref[pl.ds(kind * 2, 2), 0].reshape(ROW, HD))
    if levels > 0:
        blocks.append(ref[pl.ds(kind * 2, 2), 1 : 1 + levels].reshape(levels * ROW, HD))
    return blocks


def causal_mask(source_i):
    rows = lax.broadcasted_iota(jnp.int32, (ROW, HALF), 1)
    spots = lax.broadcasted_iota(jnp.int32, (ROW, HALF), 0)
    key_rows = ((spots & 56) << 2) + ((spots >> 6) << 4) + (spots & 7)
    return rows >= key_rows + source_i * STRIP


def attend_kernel(begins, ends, near_count, far_count, facts_ref, queries_ref, *refs):
    chunk_count = near_count + far_count
    chunks, rest = refs[:chunk_count], refs[chunk_count:]
    state, outs = ((), rest) if begins else (rest[:2], rest[2:])
    half = lax.axis_index("zl")
    own_i = lax.axis_index("i")
    count = facts_ref[0]
    causal = causal_mask(own_i if begins else 1 - own_i) if near_count else None
    positions = half * HALF + lax.broadcasted_iota(jnp.int32, (1, HALF), 1)
    valid = positions < facts_ref[1]

    def finish(head, top, total, summed):
        if ends:
            result = summed * jnp.where(valid, 1.0 / total, 0.0)
            outs[0][:, head * HD : (head + 1) * HD] = result.astype(jnp.bfloat16).T
        else:
            save(*outs, head, top, total, summed)

    def stored(head):
        return state[1][head, pl.ds(0, 8)][:1], state[1][head, pl.ds(8, 8)][:1], state[0][head]

    def body(levels, second):
        def rows_of(kind):
            blocks = []
            for index, chunk in enumerate(chunks):
                blocks += chunk_rows(chunk, kind, index < near_count or second, levels)
            return blocks

        if not rows_of(0):
            for head in range(HEADS):
                finish(head, *stored(head))
            return
        keys, values = (jnp.concatenate(rows_of(kind), axis=0) for kind in range(2))
        parts = partial_attention(head_queries(queries_ref), keys, values, causal)
        for head, (top2, total2, summed2) in enumerate(parts):
            if begins:
                finish(head, top2, total2, summed2)
                continue
            top, total, summed = stored(head)
            newest = jnp.maximum(top, top2)
            shrink = jnp.exp2((top - newest) * EXP_FACTOR)
            shrink2 = jnp.exp2((top2 - newest) * EXP_FACTOR)
            finish(head, newest, total * shrink + total2 * shrink2, summed * shrink + summed2 * shrink2)

    for levels in range(LEVELS + 1):
        if far_count == 0:
            pl.when(count == levels)(functools.partial(body, levels, False))
            continue
        for second in (False, True):
            here = (count == levels) & (half == (1 if second else 0))
            pl.when(here)(functools.partial(body, levels, second))


def on_device(queries, keys, values, parent, owner, lengths):
    bf16, f32 = jnp.bfloat16, jnp.float32
    params = pltpu.CompilerParams(vmem_limit_bytes=32 * 1024 * 1024)
    work = pl.CostEstimate(
        flops=4 * HEADS * HALF * HD * 1024, bytes_accessed=4 * 1024 * 1024, transcendentals=HEADS * HALF * 1024
    )
    small = pltpu.CompilerParams(vmem_limit_bytes=4 * 1024 * 1024)
    packed, facts = pl.pallas_call(
        pack_kernel,
        out_shape=[
            jax.ShapeDtypeStruct((4, HEADS, 2 * STRIP, HD), bf16),
            jax.ShapeDtypeStruct((TABLE + PLACES * (1 + LEVELS),), jnp.int32),
        ],
        in_specs=[SMEM, SMEM, SMEM, VMEM, VMEM],
        out_specs=[VMEM, SMEM],
        scratch_shapes=[pltpu.SMEM((SPANS,), jnp.int32)],
        name="pack_heads",
    )(parent, owner, lengths, keys, values)
    spread = lax.all_to_all(packed.reshape(64, STRIP, HD), ("x", "y", "c", "i"), 0, 0, tiled=True)
    gathered = lax.all_gather(spread.reshape(4, HEADS, 2, STRIP, HD), "zb", axis=0, tiled=True)
    picked = pl.pallas_call(
        pick_kernel,
        out_shape=jax.ShapeDtypeStruct((4, 2, 1 + LEVELS, HEADS, STRIP, HD), bf16),
        in_specs=[SMEM, VMEM],
        out_specs=VMEM,
        compiler_params=small,
        name="pick_ancestors",
    )(facts, gathered)
    passed = lax.all_to_all(picked.reshape(4, 2, 1 + LEVELS, SHARE, HD), "x", 0, 0, tiled=True)
    ours, beside = passed[:, 0], passed[:, 1]
    ring = ("zb", "i", "zl")
    far = lax.ppermute(ours, ring, [(z, z ^ 1) for z in range(16)])
    further = lax.ppermute(beside, ring, [(z, (z + (1 if z % 2 else -1)) % 16) for z in range(16)])
    state = [jax.ShapeDtypeStruct((HEADS, HD, HALF), f32), jax.ShapeDtypeStruct((HEADS, 16, HALF), f32)]

    def attend(name, begins, ends, near_count, far_count, *operands):
        return pl.pallas_call(
            functools.partial(attend_kernel, begins, ends, near_count, far_count),
            out_shape=jax.ShapeDtypeStruct((HALF, HEADS * HD), bf16) if ends else state,
            in_specs=[SMEM] + [VMEM] * (1 + len(operands)),
            out_specs=VMEM if ends else [VMEM, VMEM],
            compiler_params=params,
            cost_estimate=work,
            name=name,
        )(facts, queries, *operands)

    running = attend("attend_own", True, False, 1, 0, ours)
    beside, running = lax.optimization_barrier((beside, running))
    near = lax.ppermute(beside, ring, [(z, (z + (2 if z % 2 else -2)) % 16) for z in range(16)])
    running = attend("attend_middle", False, False, 0, 2, far, further, *running)
    return attend("attend_last", False, True, 1, 0, near, *running)


def solution(mesh):
    fine = Mesh(mesh.devices.reshape(4, 4, 2, 2, 4, 2), ("x", "zb", "i", "zl", "y", "c"))
    span, head = ("x", "zb", "i", "zl"), ("y", "c")
    return jax.shard_map(
        on_device,
        mesh=fine,
        in_specs=(P(span, head), P(span + head, None), P(span + head, None), P(), P(), P()),
        out_specs=P(span, head),
        check_vma=False,
    )
```

```python
import functools

import jax
import jax.numpy as jnp
from jax import lax
from jax.experimental import pallas as pl
from jax.experimental.pallas import tpu as pltpu
from jax.sharding import Mesh, PartitionSpec as P

HD = 128
HEADS = 8
HALF = 256
SPANS = 32
LEVELS = 3
PLACES = 8
STRIP = 8
SHARE = HEADS * STRIP
TABLE = 8
ROW = 128
HIDDEN = -1e30
EXP_FACTOR = HD ** (-0.5) * 1.4426950408889634

VMEM = pl.BlockSpec(memory_space=pltpu.VMEM)
SMEM = pl.BlockSpec(memory_space=pltpu.SMEM)


def pack_kernel(parent_ref, owner_ref, lengths_ref, keys_ref, values_ref, out_ref, facts_ref, span_at_ref):
    for kind, ref in enumerate((keys_ref, values_ref)):
        for part in range(2):
            for head in range(HEADS):
                out_ref[kind * 2 + part, head] = ref[pl.ds(part * 16, 16), pl.ds(head * HD, HD)]
    half = lax.axis_index("zl")
    pair = lax.axis_index("zb") * 2 + lax.axis_index("i")
    mine = lax.axis_index("x")
    beside = (pair + 7 + half * 2) & 7
    for span in range(SPANS):
        span_at_ref[owner_ref[span]] = span
    my_count = jnp.int32(0)
    my_length = jnp.int32(0)
    for x in range(4):
        for side in range(2):
            slot = x * 8 + (pair if side == 0 else beside)
            current = span_at_ref[slot]
            length = lengths_ref[current]
            count = jnp.int32(0)
            entry = TABLE + (x * 2 + side) * (1 + LEVELS)
            facts_ref[entry] = ((slot >> 1) & 3) * PLACES + (slot >> 3) * 2 + (slot & 1)
            for level in range(LEVELS):
                current = jnp.where(current >= 0, parent_ref[jnp.maximum(current, 0)], -1)
                count = count + jnp.where(current >= 0, 1, 0)
                slot = owner_ref[jnp.maximum(current, 0)]
                facts_ref[entry + 1 + level] = ((slot >> 1) & 3) * PLACES + (slot >> 3) * 2 + (slot & 1)
            if side == 0:
                my_count = jnp.where(mine == x, count, my_count)
                my_length = jnp.where(mine == x, length, my_length)
    facts_ref[0] = my_count
    facts_ref[1] = my_length


def pick_kernel(facts_ref, gathered_ref, out_ref):
    for x in range(4):
        for side in range(2):
            for level in range(1 + LEVELS):
                source = facts_ref[TABLE + (x * 2 + side) * (1 + LEVELS) + level]
                out_ref[x, side, level] = gathered_ref[source >> 1, :, source & 1]


def partial_attention(queries, keys, values, causal):
    all_scores = [
        lax.dot_general(keys, query, (((1,), (1,)), ((), ())), preferred_element_type=jnp.float32)
        for query in queries
    ]
    for scores in all_scores:
        if causal is not None:
            masked = jnp.where(causal, scores[:ROW], HIDDEN)
            scores = jnp.concatenate([masked, scores[ROW:]], axis=0) if scores.shape[0] > ROW else masked
        top = jnp.max(scores, axis=0, keepdims=True)
        weights = jnp.exp2((scores - top) * EXP_FACTOR)
        total = jnp.sum(weights, axis=0, keepdims=True)
        summed = lax.dot_general(
            values, weights.astype(jnp.bfloat16), (((0,), (0,)), ((), ())), preferred_element_type=jnp.float32
        )
        yield top, total, summed


def save(summed_ref, stats_ref, head, top, total, summed):
    summed_ref[head] = summed
    stats_ref[head, pl.ds(0, 8)] = jnp.broadcast_to(top, (8, HALF))
    stats_ref[head, pl.ds(8, 8)] = jnp.broadcast_to(total, (8, HALF))


def head_queries(queries_ref):
    return [queries_ref[:, head * HD : (head + 1) * HD] for head in range(HEADS)]


def chunk_rows(ref, kind, with_own, levels):
    blocks = []
    if with_own:
        blocks.append(ref[pl.ds(kind * 2, 2), 0].reshape(ROW, HD))
    if levels > 0:
        blocks.append(ref[pl.ds(kind * 2, 2), 1 : 1 + levels].reshape(levels * ROW, HD))
    return blocks


def causal_mask(source_i):
    rows = lax.broadcasted_iota(jnp.int32, (ROW, HALF), 1)
    spots = lax.broadcasted_iota(jnp.int32, (ROW, HALF), 0)
    key_rows = ((spots & 56) << 2) + ((spots >> 6) << 4) + (spots & 7)
    return rows >= key_rows + source_i * STRIP


def attend_kernel(begins, ends, near_count, far_count, facts_ref, queries_ref, *refs):
    chunk_count = near_count + far_count
    chunks, rest = refs[:chunk_count], refs[chunk_count:]
    state, outs = ((), rest) if begins else (rest[:2], rest[2:])
    half = lax.axis_index("zl")
    own_i = lax.axis_index("i")
    count = facts_ref[0]
    causal = causal_mask(own_i if begins else 1 - own_i) if near_count else None
    positions = half * HALF + lax.broadcasted_iota(jnp.int32, (1, HALF), 1)
    valid = positions < facts_ref[1]

    def copy_out(group):
        columns = pl.ds(group * 2 * HD, 2 * HD)
        return pltpu.make_async_copy(outs[1].at[:, columns], outs[0].at[:, columns], outs[2].at[group])

    def finish(head, top, total, summed):
        if ends:
            result = summed * jnp.where(valid, 1.0 / total, 0.0)
            outs[1][:, head * HD : (head + 1) * HD] = result.astype(jnp.bfloat16).T
            if head % 2 == 1:
                copy_out(head // 2).start()
        else:
            save(*outs, head, top, total, summed)

    def stored(head):
        return state[1][head, pl.ds(0, 8)][:1], state[1][head, pl.ds(8, 8)][:1], state[0][head]

    def body(levels, second):
        def rows_of(kind):
            blocks = []
            for index, chunk in enumerate(chunks):
                blocks += chunk_rows(chunk, kind, index < near_count or second, levels)
            return blocks

        if not rows_of(0):
            for head in range(HEADS):
                finish(head, *stored(head))
            settle()
            return
        keys, values = (jnp.concatenate(rows_of(kind), axis=0) for kind in range(2))
        parts = partial_attention(head_queries(queries_ref), keys, values, causal)
        for head, (top2, total2, summed2) in enumerate(parts):
            if begins:
                finish(head, top2, total2, summed2)
                continue
            top, total, summed = stored(head)
            newest = jnp.maximum(top, top2)
            shrink = jnp.exp2((top - newest) * EXP_FACTOR)
            shrink2 = jnp.exp2((top2 - newest) * EXP_FACTOR)
            finish(head, newest, total * shrink + total2 * shrink2, summed * shrink + summed2 * shrink2)
        settle()

    def settle():
        if ends:
            for group in range(HEADS // 2):
                copy_out(group).wait()

    for levels in range(LEVELS + 1):
        if far_count == 0:
            pl.when(count == levels)(functools.partial(body, levels, False))
            continue
        for second in (False, True):
            here = (count == levels) & (half == (1 if second else 0))
            pl.when(here)(functools.partial(body, levels, second))


def on_device(queries, keys, values, parent, owner, lengths):
    bf16, f32 = jnp.bfloat16, jnp.float32
    params = pltpu.CompilerParams(vmem_limit_bytes=32 * 1024 * 1024)
    work = pl.CostEstimate(
        flops=4 * HEADS * HALF * HD * 1024, bytes_accessed=4 * 1024 * 1024, transcendentals=HEADS * HALF * 1024
    )
    small = pltpu.CompilerParams(vmem_limit_bytes=4 * 1024 * 1024)
    packed, facts = pl.pallas_call(
        pack_kernel,
        out_shape=[
            jax.ShapeDtypeStruct((4, HEADS, 2 * STRIP, HD), bf16),
            jax.ShapeDtypeStruct((TABLE + PLACES * (1 + LEVELS),), jnp.int32),
        ],
        in_specs=[SMEM, SMEM, SMEM, VMEM, VMEM],
        out_specs=[VMEM, SMEM],
        scratch_shapes=[pltpu.SMEM((SPANS,), jnp.int32)],
        name="pack_heads",
    )(parent, owner, lengths, keys, values)
    spread = lax.all_to_all(packed.reshape(64, STRIP, HD), ("x", "y", "c", "i"), 0, 0, tiled=True)
    gathered = lax.all_gather(spread.reshape(4, HEADS, 2, STRIP, HD), "zb", axis=0, tiled=True)
    picked = pl.pallas_call(
        pick_kernel,
        out_shape=jax.ShapeDtypeStruct((4, 2, 1 + LEVELS, HEADS, STRIP, HD), bf16),
        in_specs=[SMEM, VMEM],
        out_specs=VMEM,
        compiler_params=small,
        name="pick_ancestors",
    )(facts, gathered)
    passed = lax.all_to_all(picked.reshape(4, 2, 1 + LEVELS, SHARE, HD), "x", 0, 0, tiled=True)
    ours, beside = passed[:, 0], passed[:, 1]
    ring = ("zb", "i", "zl")
    far = lax.ppermute(ours, ring, [(z, z ^ 1) for z in range(16)])
    further = lax.ppermute(beside, ring, [(z, (z + (1 if z % 2 else -1)) % 16) for z in range(16)])
    state = [jax.ShapeDtypeStruct((HEADS, HD, HALF), f32), jax.ShapeDtypeStruct((HEADS, 16, HALF), f32)]

    def attend(name, begins, ends, near_count, far_count, *operands):
        return pl.pallas_call(
            functools.partial(attend_kernel, begins, ends, near_count, far_count),
            out_shape=jax.ShapeDtypeStruct((HALF, HEADS * HD), bf16) if ends else state,
            in_specs=[SMEM] + [VMEM] * (1 + len(operands)),
            out_specs=pl.BlockSpec(memory_space=pl.ANY) if ends else [VMEM, VMEM],
            scratch_shapes=[pltpu.VMEM((HALF, HEADS * HD), bf16), pltpu.SemaphoreType.DMA((HEADS // 2,))]
            if ends
            else [],
            compiler_params=params,
            cost_estimate=work,
            name=name,
        )(facts, queries, *operands)

    running = attend("attend_own", True, False, 1, 0, ours)
    beside, running = lax.optimization_barrier((beside, running))
    near = lax.ppermute(beside, ring, [(z, (z + (2 if z % 2 else -2)) % 16) for z in range(16)])
    running = attend("attend_middle", False, False, 0, 2, far, further, *running)
    return attend("attend_last", False, True, 1, 0, near, *running)


def solution(mesh):
    fine = Mesh(mesh.devices.reshape(4, 4, 2, 2, 4, 2), ("x", "zb", "i", "zl", "y", "c"))
    span, head = ("x", "zb", "i", "zl"), ("y", "c")
    return jax.shard_map(
        on_device,
        mesh=fine,
        in_specs=(P(span, head), P(span + head, None), P(span + head, None), P(), P(), P()),
        out_specs=P(span, head),
        check_vma=False,
    )
```

```python
import functools

import jax
import jax.numpy as jnp
from jax import lax
from jax.experimental import pallas as pl
from jax.experimental.pallas import tpu as pltpu
from jax.sharding import Mesh, PartitionSpec as P

HD = 128
HEADS = 8
HALF = 256
SPANS = 32
LEVELS = 3
PLACES = 8
STRIP = 8
SHARE = HEADS * STRIP
TABLE = 8
ROW = 128
HIDDEN = -1e30
EXP_FACTOR = HD ** (-0.5) * 1.4426950408889634

VMEM = pl.BlockSpec(memory_space=pltpu.VMEM)
SMEM = pl.BlockSpec(memory_space=pltpu.SMEM)


def pack_kernel(parent_ref, owner_ref, lengths_ref, keys_ref, values_ref, out_ref, facts_ref, span_at_ref):
    for kind, ref in enumerate((keys_ref, values_ref)):
        for part in range(2):
            for head in range(HEADS):
                out_ref[kind * 2 + part, head] = ref[pl.ds(part * 16, 16), pl.ds(head * HD, HD)]
    half = lax.axis_index("zl")
    pair = lax.axis_index("zb") * 2 + lax.axis_index("i")
    mine = lax.axis_index("x")
    beside = (pair + 7 + half * 2) & 7
    for span in range(SPANS):
        span_at_ref[owner_ref[span]] = span
    my_count = jnp.int32(0)
    my_length = jnp.int32(0)
    for x in range(4):
        for side in range(2):
            slot = x * 8 + (pair if side == 0 else beside)
            current = span_at_ref[slot]
            length = lengths_ref[current]
            count = jnp.int32(0)
            entry = TABLE + (x * 2 + side) * (1 + LEVELS)
            facts_ref[entry] = ((slot >> 1) & 3) * PLACES + (slot >> 3) * 2 + (slot & 1)
            for level in range(LEVELS):
                current = jnp.where(current >= 0, parent_ref[jnp.maximum(current, 0)], -1)
                count = count + jnp.where(current >= 0, 1, 0)
                slot = owner_ref[jnp.maximum(current, 0)]
                facts_ref[entry + 1 + level] = ((slot >> 1) & 3) * PLACES + (slot >> 3) * 2 + (slot & 1)
            if side == 0:
                my_count = jnp.where(mine == x, count, my_count)
                my_length = jnp.where(mine == x, length, my_length)
    facts_ref[0] = my_count
    facts_ref[1] = my_length


def pick_kernel(facts_ref, gathered_ref, out_ref):
    for x in range(4):
        for side in range(2):
            for level in range(1 + LEVELS):
                source = facts_ref[TABLE + (x * 2 + side) * (1 + LEVELS) + level]
                out_ref[x, side, level] = gathered_ref[source >> 1, :, source & 1]


def partial_attention(queries, keys, values, causal):
    all_scores = [
        lax.dot_general(keys, query, (((1,), (1,)), ((), ())), preferred_element_type=jnp.float32)
        for query in queries
    ]
    for scores in all_scores:
        if causal is not None:
            masked = jnp.where(causal, scores[:ROW], HIDDEN)
            scores = jnp.concatenate([masked, scores[ROW:]], axis=0) if scores.shape[0] > ROW else masked
        top = jnp.max(scores, axis=0, keepdims=True)
        weights = jnp.exp2((scores - top) * EXP_FACTOR)
        total = jnp.sum(weights, axis=0, keepdims=True)
        summed = lax.dot_general(
            values, weights.astype(jnp.bfloat16), (((0,), (0,)), ((), ())), preferred_element_type=jnp.float32
        )
        yield top, total, summed


def save(summed_ref, stats_ref, head, top, total, summed):
    summed_ref[head] = summed
    stats_ref[head, pl.ds(0, 8)] = jnp.broadcast_to(top, (8, HALF))
    stats_ref[head, pl.ds(8, 8)] = jnp.broadcast_to(total, (8, HALF))


def head_queries(queries_ref):
    return [queries_ref[:, head * HD : (head + 1) * HD] for head in range(HEADS)]


def chunk_rows(ref, kind, with_own, levels):
    blocks = []
    if with_own:
        blocks.append(ref[pl.ds(kind * 2, 2), 0].reshape(ROW, HD))
    if levels > 0:
        blocks.append(ref[pl.ds(kind * 2, 2), 1 : 1 + levels].reshape(levels * ROW, HD))
    return blocks


def causal_mask(source_i):
    rows = lax.broadcasted_iota(jnp.int32, (ROW, HALF), 1)
    spots = lax.broadcasted_iota(jnp.int32, (ROW, HALF), 0)
    key_rows = ((spots & 56) << 2) + ((spots >> 6) << 4) + (spots & 7)
    return rows >= key_rows + source_i * STRIP


def attend_kernel(begins, ends, near_count, far_count, facts_ref, queries_ref, *refs):
    chunk_count = near_count + far_count
    chunks, rest = refs[:chunk_count], refs[chunk_count:]
    state, outs = ((), rest) if begins else (rest[:2], rest[2:])
    half = lax.axis_index("zl")
    own_i = lax.axis_index("i")
    count = facts_ref[0]
    causal = causal_mask(own_i if begins else 1 - own_i) if near_count else None
    positions = half * HALF + lax.broadcasted_iota(jnp.int32, (1, HALF), 1)
    valid = positions < facts_ref[1]

    def finish(head, top, total, summed):
        if ends:
            result = summed * jnp.where(valid, 1.0 / total, 0.0)
            outs[0][:, head * HD : (head + 1) * HD] = result.astype(jnp.bfloat16).T
        else:
            save(*outs, head, top, total, summed)

    def stored(head):
        return state[1][head, pl.ds(0, 8)][:1], state[1][head, pl.ds(8, 8)][:1], state[0][head]

    def body(levels, second):
        def rows_of(kind):
            blocks = []
            for index, chunk in enumerate(chunks):
                blocks += chunk_rows(chunk, kind, index < near_count or second, levels)
            return blocks

        if not rows_of(0):
            for head in range(HEADS):
                finish(head, *stored(head))
            return
        keys, values = (jnp.concatenate(rows_of(kind), axis=0) for kind in range(2))
        parts = partial_attention(head_queries(queries_ref), keys, values, causal)
        for head, (top2, total2, summed2) in enumerate(parts):
            if begins:
                finish(head, top2, total2, summed2)
                continue
            top, total, summed = stored(head)
            newest = jnp.maximum(top, top2)
            shrink = jnp.exp2((top - newest) * EXP_FACTOR)
            shrink2 = jnp.exp2((top2 - newest) * EXP_FACTOR)
            finish(head, newest, total * shrink + total2 * shrink2, summed * shrink + summed2 * shrink2)

    for levels in range(LEVELS + 1):
        if far_count == 0:
            pl.when(count == levels)(functools.partial(body, levels, False))
            continue
        for second in (False, True):
            here = (count == levels) & (half == (1 if second else 0))
            pl.when(here)(functools.partial(body, levels, second))


def on_device(queries, keys, values, parent, owner, lengths):
    bf16, f32 = jnp.bfloat16, jnp.float32
    params = pltpu.CompilerParams(vmem_limit_bytes=32 * 1024 * 1024)
    work = pl.CostEstimate(
        flops=4 * HEADS * HALF * HD * 1024, bytes_accessed=4 * 1024 * 1024, transcendentals=HEADS * HALF * 1024
    )
    small = pltpu.CompilerParams(vmem_limit_bytes=4 * 1024 * 1024)
    packed, facts = pl.pallas_call(
        pack_kernel,
        out_shape=[
            jax.ShapeDtypeStruct((4, HEADS, 2 * STRIP, HD), bf16),
            jax.ShapeDtypeStruct((TABLE + PLACES * (1 + LEVELS),), jnp.int32),
        ],
        in_specs=[SMEM, SMEM, SMEM, VMEM, VMEM],
        out_specs=[VMEM, SMEM],
        scratch_shapes=[pltpu.SMEM((SPANS,), jnp.int32)],
        name="pack_heads",
    )(parent, owner, lengths, keys, values)
    spread = lax.all_to_all(packed.reshape(64, STRIP, HD), ("x", "y", "c", "i"), 0, 0, tiled=True)
    gathered = lax.all_gather(spread.reshape(4, HEADS, 2, STRIP, HD), "zb", axis=0, tiled=True)
    picked = pl.pallas_call(
        pick_kernel,
        out_shape=jax.ShapeDtypeStruct((4, 2, 1 + LEVELS, HEADS, STRIP, HD), bf16),
        in_specs=[SMEM, VMEM],
        out_specs=VMEM,
        compiler_params=small,
        name="pick_ancestors",
    )(facts, gathered)
    passed = lax.all_to_all(picked.reshape(4, 2, 1 + LEVELS, SHARE, HD), "x", 0, 0, tiled=True)
    ours, beside = passed[:, 0], passed[:, 1]
    ring = ("zb", "i", "zl")
    far = lax.ppermute(ours, ring, [(z, z ^ 1) for z in range(16)])
    further = lax.ppermute(beside, ring, [(z, (z + (1 if z % 2 else -1)) % 16) for z in range(16)])
    state = [jax.ShapeDtypeStruct((HEADS, HD, HALF), f32), jax.ShapeDtypeStruct((HEADS, 16, HALF), f32)]

    def attend(name, begins, ends, near_count, far_count, *operands):
        return pl.pallas_call(
            functools.partial(attend_kernel, begins, ends, near_count, far_count),
            out_shape=jax.ShapeDtypeStruct((HALF, HEADS * HD), bf16) if ends else state,
            in_specs=[SMEM] + [VMEM] * (1 + len(operands)),
            out_specs=VMEM if ends else [VMEM, VMEM],
            compiler_params=params,
            cost_estimate=work,
            name=name,
        )(facts, queries, *operands)

    running = attend("attend_own", True, False, 1, 0, ours)

    near = lax.ppermute(beside, ring, [(z, (z + (2 if z % 2 else -2)) % 16) for z in range(16)])
    running = attend("attend_middle", False, False, 0, 2, far, further, *running)
    return attend("attend_last", False, True, 1, 0, near, *running)


def solution(mesh):
    fine = Mesh(mesh.devices.reshape(4, 4, 2, 2, 4, 2), ("x", "zb", "i", "zl", "y", "c"))
    span, head = ("x", "zb", "i", "zl"), ("y", "c")
    return jax.shard_map(
        on_device,
        mesh=fine,
        in_specs=(P(span, head), P(span + head, None), P(span + head, None), P(), P(), P()),
        out_specs=P(span, head),
        check_vma=False,
    )
```
